32 devices in a mesh: groups: 2 (over y), res: 16 (over z, x, core).
Axes of the slice: x: 2, y: 2, z: 4, core: 2. Of those that a mesh axis runs over, the one named last changes fastest.
Arguments:
- homolog_embedding: bfloat16 [512, 64, 256], P('groups', 'res'), parts along dimension 0, may hold values from -6 to 6
- pair_state: bfloat16 [128, 64, 128], P(('groups', 'res')), parts along dimension 0, may hold values from -6 to 6
- homolog_norm_scale: float32 [256], replicated, may hold values from 0.25 to 1.75
- former_operand_matrix: bfloat16 [256, 32], replicated, may hold values from -0.375 to 0.375
- latter_operand_matrix: bfloat16 [256, 32], replicated, may hold values from -0.375 to 0.375
- outer_mean_weight: bfloat16 [1024, 128], replicated, may hold values from -0.1875 to 0.1875
- outer_mean_bias: float32 [128], replicated, may hold values from -3 to 3
- outgoing_input_gain: float32 [128], replicated, may hold values from 0.25 to 1.75
- outgoing_edge_weight: bfloat16 [128, 256], replicated, may hold values from -0.5 to 0.5
- outgoing_gate_weight: bfloat16 [128, 128], replicated, may hold values from -0.5 to 0.5
- outgoing_product_gain: float32 [64], replicated, may hold values from 0.25 to 1.75
- outgoing_output_weight: bfloat16 [64, 128], replicated, may hold values from -0.75 to 0.75
- incoming_input_gain: float32 [128], replicated, may hold values from 0.25 to 1.75
- incoming_edge_weight: bfloat16 [128, 256], replicated, may hold values from -0.5 to 0.5
- incoming_gate_weight: bfloat16 [128, 128], replicated, may hold values from -0.5 to 0.5
- incoming_product_gain: float32 [64], replicated, may hold values from 0.25 to 1.75
- incoming_output_weight: bfloat16 [64, 128], replicated, may hold values from -0.75 to 0.75
Outputs:
- pair_three: bfloat16 [128, 64, 128], P(('groups', 'res')), parts along dimension 0
The draws below stay inside these ranges and needn't reach their ends.
There are 2 independent parts, one for each index of `groups`. The reference program is written for one: setup_inputs(seed, part) draws one part's arguments, and reference() takes and returns one part's arrays. A program takes and returns all parts, laid end to end along the dimension named above; an argument that names none is the same for every part. Nothing has to cross between parts.
All inputs are finite; a program needn't handle non-finite values.
Results may differ from the reference program's by a relative error of at most 0.013.
Values may be sent and summed in bfloat16 or wider, within the bound.
A program may use at most 128 MiB of HBM per device.

```python
import jax
import jax.numpy as jnp
from jax import lax

HOMOLOG_TOTAL = 256
ALIGNED_CHANNELS = 256
C = 128
PROJ_CHANNELS = 32
CT = 64
CHAIN_LENGTH = 64


def levels(rng, shape, cuts, least, top_value):
    factor_of, own = 1.0, jax.random.fold_in(rng, 6)
    for dim, shards_of in cuts:
        draws = jnp.exp(jax.random.uniform(jax.random.fold_in(own, dim), (shards_of,), jnp.float32, least / len(cuts), top_value / len(cuts)))
        factor_of = factor_of * jnp.repeat(draws, shape[dim] // shards_of).reshape([-1 if axis == dim else 1 for axis in range(len(shape))])
    return factor_of


def bell_draw(rng, dims, spread, bound, split=(), held_as=jnp.bfloat16):
    drawn = spread * jax.random.normal(rng, dims, jnp.float32)
    if split:
        drawn = drawn * levels(rng, dims, split, -0.22, 0.18)
    return jnp.clip(drawn, -bound, bound).astype(held_as)


def setup_inputs(seed: int = 0, part: int = 0) -> dict:
    arg_keys = jax.random.split(jax.random.key(seed), 18)
    own_keys = jax.random.split(jax.random.fold_in(arg_keys[17], part), 18)
    homolog_embedding = bell_draw(own_keys[0], (HOMOLOG_TOTAL, CHAIN_LENGTH, ALIGNED_CHANNELS), 1.0, 6.0, ((1, 16),))
    pair_state = bell_draw(own_keys[1], (CHAIN_LENGTH, CHAIN_LENGTH, C), 1.0, 6.0, ((0, 16),))
    homolog_norm_scale = jnp.clip(1.0 + 0.15 * jax.random.normal(arg_keys[2], (ALIGNED_CHANNELS,), jnp.float32), 0.25, 1.75)
    former_operand_matrix = bell_draw(arg_keys[3], (ALIGNED_CHANNELS, PROJ_CHANNELS), ALIGNED_CHANNELS ** -0.5, 0.375)
    latter_operand_matrix = bell_draw(arg_keys[4], (ALIGNED_CHANNELS, PROJ_CHANNELS), ALIGNED_CHANNELS ** -0.5, 0.375)
    outer_mean_weight = bell_draw(arg_keys[5], (PROJ_CHANNELS * PROJ_CHANNELS, C), (PROJ_CHANNELS * PROJ_CHANNELS) ** -0.5, 0.1875)
    outer_mean_bias = bell_draw(arg_keys[6], (C,), 0.5, 3.0, (), jnp.float32)
    outgoing_input_gain = jnp.clip(1.0 + 0.15 * jax.random.normal(arg_keys[7], (C,), jnp.float32), 0.25, 1.75)
    outgoing_edge_weight = bell_draw(arg_keys[8], (C, 4 * CT), C ** -0.5, 0.5)
    outgoing_gate_weight = bell_draw(arg_keys[9], (C, C), C ** -0.5, 0.5)
    outgoing_product_gain = jnp.clip(1.0 + 0.15 * jax.random.normal(arg_keys[10], (CT,), jnp.float32), 0.25, 1.75)
    outgoing_output_weight = bell_draw(arg_keys[11], (CT, C), CT ** -0.5, 0.75)
    incoming_input_gain = jnp.clip(1.0 + 0.15 * jax.random.normal(arg_keys[12], (C,), jnp.float32), 0.25, 1.75)
    incoming_edge_weight = bell_draw(arg_keys[13], (C, 4 * CT), C ** -0.5, 0.5)
    incoming_gate_weight = bell_draw(arg_keys[14], (C, C), C ** -0.5, 0.5)
    incoming_product_gain = jnp.clip(1.0 + 0.15 * jax.random.normal(arg_keys[15], (CT,), jnp.float32), 0.25, 1.75)
    incoming_output_weight = bell_draw(arg_keys[16], (CT, C), CT ** -0.5, 0.75)
    return {"homolog_embedding": homolog_embedding, "pair_state": pair_state, "homolog_norm_scale": homolog_norm_scale, "former_operand_matrix": former_operand_matrix, "latter_operand_matrix": latter_operand_matrix, "outer_mean_weight": outer_mean_weight, "outer_mean_bias": outer_mean_bias, "outgoing_input_gain": outgoing_input_gain, "outgoing_edge_weight": outgoing_edge_weight, "outgoing_gate_weight": outgoing_gate_weight, "outgoing_product_gain": outgoing_product_gain, "outgoing_output_weight": outgoing_output_weight, "incoming_input_gain": incoming_input_gain, "incoming_edge_weight": incoming_edge_weight, "incoming_gate_weight": incoming_gate_weight, "incoming_product_gain": incoming_product_gain, "incoming_output_weight": incoming_output_weight}


def layer_normalize(values, gain):
    mean_val = lax.optimization_barrier(jnp.mean(values, axis=-1, keepdims=True))
    centred = values - mean_val
    variance = lax.optimization_barrier(jnp.mean(centred * centred, axis=-1, keepdims=True))
    return centred / jnp.sqrt(variance + 1e-05) * gain

def triangle(pair_block, norm_gain, weight_in, weight_gate, mid_gain, weight_final, form):
    hidden_width = weight_in.shape[1] // 4
    normed = layer_normalize(pair_block.astype(jnp.float32), norm_gain).astype(jnp.bfloat16)
    projected = jnp.einsum('ijc,cd->ijd', normed.astype(jnp.float32), weight_in.astype(jnp.float32))
    edge_a = (jax.nn.sigmoid(projected[..., hidden_width:2 * hidden_width]) * projected[..., :hidden_width]).astype(jnp.bfloat16)
    edge_b = (jax.nn.sigmoid(projected[..., 3 * hidden_width:]) * projected[..., 2 * hidden_width:3 * hidden_width]).astype(jnp.bfloat16)
    gating = jax.nn.sigmoid(jnp.einsum('ijc,cd->ijd', normed.astype(jnp.float32), weight_gate.astype(jnp.float32)))
    mixed = jnp.einsum(form, edge_a.astype(jnp.float32), edge_b.astype(jnp.float32))
    mixed_normed = layer_normalize(mixed, mid_gain).astype(jnp.bfloat16)
    update = jnp.einsum('ijc,cd->ijd', mixed_normed.astype(jnp.float32), weight_final.astype(jnp.float32))
    return (pair_block.astype(jnp.float32) + gating * update).astype(jnp.bfloat16)

def reference(homolog_embedding, pair_state, homolog_norm_scale, former_operand_matrix, latter_operand_matrix, outer_mean_weight, outer_mean_bias, outgoing_input_gain, outgoing_edge_weight, outgoing_gate_weight, outgoing_product_gain, outgoing_output_weight, incoming_input_gain, incoming_edge_weight, incoming_gate_weight, incoming_product_gain, incoming_output_weight):
    alignment_normalized = layer_normalize(homolog_embedding.astype(jnp.float32), homolog_norm_scale).astype(jnp.bfloat16)
    left_factor = jnp.einsum('vfd,dl->vfl', alignment_normalized.astype(jnp.float32), former_operand_matrix.astype(jnp.float32)).astype(jnp.bfloat16)
    right_factor = jnp.einsum('vfd,dl->vfl', alignment_normalized.astype(jnp.float32), latter_operand_matrix.astype(jnp.float32)).astype(jnp.bfloat16)
    outer = jnp.einsum('sip,sjq->ijpq', left_factor.astype(jnp.float32), right_factor.astype(jnp.float32)) / HOMOLOG_TOTAL
    outer = outer.reshape(CHAIN_LENGTH, CHAIN_LENGTH, PROJ_CHANNELS * PROJ_CHANNELS).astype(jnp.bfloat16)
    update = jnp.einsum('ijr,rc->ijc', outer.astype(jnp.float32), outer_mean_weight.astype(jnp.float32)) + outer_mean_bias
    pair_one = (pair_state.astype(jnp.float32) + update).astype(jnp.bfloat16)
    pair_two = triangle(pair_one, outgoing_input_gain, outgoing_edge_weight, outgoing_gate_weight, outgoing_product_gain, outgoing_output_weight, 'ikc,jkc->ijc')
    return triangle(pair_two, incoming_input_gain, incoming_edge_weight, incoming_gate_weight, incoming_product_gain, incoming_output_weight, 'kic,kjc->ijc')
```

```python
import jax
import jax.numpy as jnp
from jax import lax
from jax.sharding import PartitionSpec as P


def layer_normalize(values, gain):
    mean_val = jnp.mean(values, axis=-1, keepdims=True)
    centred = values - mean_val
    variance = jnp.mean(centred * centred, axis=-1, keepdims=True)
    return centred / jnp.sqrt(variance + 1e-05) * gain


def project_in(pair_block, norm_gain, weight_in, weight_gate):
    hidden_width = weight_in.shape[1] // 4
    normed = layer_normalize(pair_block.astype(jnp.float32), norm_gain).astype(jnp.bfloat16)
    projected = jnp.einsum("abc,cd->abd", normed, weight_in, preferred_element_type=jnp.float32)
    edge_left = (
        jax.nn.sigmoid(projected[..., hidden_width : 2 * hidden_width])
        * projected[..., :hidden_width]
    ).astype(jnp.bfloat16)
    edge_right = (
        jax.nn.sigmoid(projected[..., 3 * hidden_width :])
        * projected[..., 2 * hidden_width : 3 * hidden_width]
    ).astype(jnp.bfloat16)
    gating = jax.nn.sigmoid(
        jnp.einsum("abc,cd->abd", normed, weight_gate, preferred_element_type=jnp.float32)
    )
    return (edge_left, edge_right, gating)


def apply_update(pair_block, gating, mixed_normed, weight_final):
    update = jnp.einsum(
        "abc,cd->abd", mixed_normed, weight_final, preferred_element_type=jnp.float32
    )
    return (pair_block.astype(jnp.float32) + gating * update).astype(jnp.bfloat16)


def shards(
    homolog_embedding,
    pair_state,
    homolog_norm_scale,
    former_operand_matrix,
    latter_operand_matrix,
    outer_mean_weight,
    outer_mean_bias,
    outgoing_input_gain,
    outgoing_edge_weight,
    outgoing_gate_weight,
    outgoing_product_gain,
    outgoing_output_weight,
    incoming_input_gain,
    incoming_edge_weight,
    incoming_gate_weight,
    incoming_product_gain,
    incoming_output_weight,
):
    sequence_rows = homolog_embedding.shape[0]
    alignment_normalized = layer_normalize(
        homolog_embedding.astype(jnp.float32), homolog_norm_scale
    ).astype(jnp.bfloat16)
    left_factor = jnp.einsum(
        "vfd,dl->vfl",
        alignment_normalized,
        former_operand_matrix,
        preferred_element_type=jnp.float32,
    ).astype(jnp.bfloat16)
    right_factor = jnp.einsum(
        "vfd,dl->vfl",
        alignment_normalized,
        latter_operand_matrix,
        preferred_element_type=jnp.float32,
    ).astype(jnp.bfloat16)
    outer = (
        jnp.einsum(
            "sip,sjq->ijpq",
            left_factor,
            lax.all_gather(right_factor, "res", axis=1, tiled=True),
            preferred_element_type=jnp.float32,
        )
        / sequence_rows
    )
    flattened = outer.reshape(outer.shape[0], outer.shape[1], -1).astype(jnp.bfloat16)
    outer_update = (
        jnp.einsum("ijr,rc->ijc", flattened, outer_mean_weight, preferred_element_type=jnp.float32)
        + outer_mean_bias
    )
    pair_one = (pair_state.astype(jnp.float32) + outer_update).astype(jnp.bfloat16)
    edge_left, edge_right, gating = project_in(
        pair_one, outgoing_input_gain, outgoing_edge_weight, outgoing_gate_weight
    )
    mixed = jnp.einsum(
        "ikc,jkc->ijc",
        edge_left,
        lax.all_gather(edge_right, "res", axis=0, tiled=True),
        preferred_element_type=jnp.float32,
    )
    mixed_normed = layer_normalize(mixed, outgoing_product_gain).astype(jnp.bfloat16)
    pair_two = apply_update(pair_one, gating, mixed_normed, outgoing_output_weight)
    in_left, in_right, in_gating = project_in(
        pair_two, incoming_input_gain, incoming_edge_weight, incoming_gate_weight
    )
    in_mixed = jnp.einsum(
        "kic,kjc->ijc",
        lax.all_to_all(in_left, "res", split_axis=1, concat_axis=0, tiled=True),
        lax.all_gather(in_right, "res", axis=0, tiled=True),
        preferred_element_type=jnp.float32,
    )
    in_normed = layer_normalize(in_mixed, incoming_product_gain).astype(jnp.bfloat16)
    return apply_update(pair_two, in_gating, in_normed, incoming_output_weight)


def solution(mesh):
    in_specs = (
        P("groups", "res", None),
        P(("groups", "res"), None, None),
        P(),
        P(),
        P(),
        P(),
        P(),
        P(),
        P(),
        P(),
        P(),
        P(),
        P(),
        P(),
        P(),
        P(),
        P(),
    )
    out_specs = P(("groups", "res"), None, None)
    return jax.shard_map(shards, mesh=mesh, in_specs=in_specs, out_specs=out_specs, check_vma=False)
```

```python
import functools

import jax
import jax.numpy as jnp
from jax import lax
from jax.experimental import pallas as pl
from jax.experimental.pallas import tpu as pltpu
from jax.sharding import PartitionSpec as P


def layer_normalize(values, gain):
    mean_val = jnp.mean(values, axis=-1, keepdims=True)
    centred = values - mean_val
    variance = jnp.mean(centred * centred, axis=-1, keepdims=True)
    return centred / jnp.sqrt(variance + 1e-05) * gain


def project_in(pair_block, norm_gain, weight_in, weight_gate):
    hidden_width = weight_in.shape[1] // 4
    normed = layer_normalize(pair_block.astype(jnp.float32), norm_gain).astype(jnp.bfloat16)
    projected = jnp.einsum("abc,cd->abd", normed, weight_in, preferred_element_type=jnp.float32)
    edge_left = (
        jax.nn.sigmoid(projected[..., hidden_width : 2 * hidden_width])
        * projected[..., :hidden_width]
    ).astype(jnp.bfloat16)
    edge_right = (
        jax.nn.sigmoid(projected[..., 3 * hidden_width :])
        * projected[..., 2 * hidden_width : 3 * hidden_width]
    ).astype(jnp.bfloat16)
    gating = jax.nn.sigmoid(
        jnp.einsum("abc,cd->abd", normed, weight_gate, preferred_element_type=jnp.float32)
    )
    return (edge_left, edge_right, gating)


def apply_update(pair_block, gating, mixed_normed, weight_final):
    update = jnp.einsum(
        "abc,cd->abd", mixed_normed, weight_final, preferred_element_type=jnp.float32
    )
    return (pair_block.astype(jnp.float32) + gating * update).astype(jnp.bfloat16)


def shards(
    homolog_embedding,
    pair_state,
    homolog_norm_scale,
    former_operand_matrix,
    latter_operand_matrix,
    outer_mean_weight,
    outer_mean_bias,
    outgoing_input_gain,
    outgoing_edge_weight,
    outgoing_gate_weight,
    outgoing_product_gain,
    outgoing_output_weight,
    incoming_input_gain,
    incoming_edge_weight,
    incoming_gate_weight,
    incoming_product_gain,
    incoming_output_weight,
):
    sequence_rows = homolog_embedding.shape[0]
    alignment_normalized = layer_normalize(
        homolog_embedding.astype(jnp.float32), homolog_norm_scale
    ).astype(jnp.bfloat16)
    left_factor = jnp.einsum(
        "vfd,dl->vfl",
        alignment_normalized,
        former_operand_matrix,
        preferred_element_type=jnp.float32,
    ).astype(jnp.bfloat16)
    right_factor = jnp.einsum(
        "vfd,dl->vfl",
        alignment_normalized,
        latter_operand_matrix,
        preferred_element_type=jnp.float32,
    ).astype(jnp.bfloat16)
    outer = (
        jnp.einsum(
            "sip,sjq->ijpq",
            left_factor,
            lax.all_gather(right_factor, "res", axis=1, tiled=True),
            preferred_element_type=jnp.float32,
        )
        / sequence_rows
    )
    flattened = outer.reshape(outer.shape[0], outer.shape[1], -1).astype(jnp.bfloat16)
    outer_update = (
        jnp.einsum("ijr,rc->ijc", flattened, outer_mean_weight, preferred_element_type=jnp.float32)
        + outer_mean_bias
    )
    pair_one = (pair_state.astype(jnp.float32) + outer_update).astype(jnp.bfloat16)
    edge_left, edge_right, gating = project_in(
        pair_one, outgoing_input_gain, outgoing_edge_weight, outgoing_gate_weight
    )
    mixed = jnp.einsum(
        "ikc,jkc->ijc",
        edge_left,
        lax.all_gather(edge_right, "res", axis=0, tiled=True),
        preferred_element_type=jnp.float32,
    )
    mixed_normed = layer_normalize(mixed, outgoing_product_gain).astype(jnp.bfloat16)
    pair_two = apply_update(pair_one, gating, mixed_normed, outgoing_output_weight)
    in_left, in_right, in_gating = project_in(
        pair_two, incoming_input_gain, incoming_edge_weight, incoming_gate_weight
    )
    in_mixed = jnp.einsum(
        "kic,kjc->ijc",
        lax.all_to_all(in_left, "res", split_axis=1, concat_axis=0, tiled=True),
        lax.all_gather(in_right, "res", axis=0, tiled=True),
        preferred_element_type=jnp.float32,
    )
    in_normed = layer_normalize(in_mixed, incoming_product_gain).astype(jnp.bfloat16)
    return apply_update(pair_two, in_gating, in_normed, incoming_output_weight)


def sigmoid(values):
    return 1.0 / (1.0 + jnp.exp(-values))


def selection(size, source_row):
    out_row = lax.broadcasted_iota(jnp.int32, (size, size), 0)
    column = lax.broadcasted_iota(jnp.int32, (size, size), 1)
    return jnp.where(source_row(out_row) == column, 1.0, 0.0).astype(jnp.bfloat16)


def field(value, low, mask, to):
    return ((value >> low) & mask) << to


def dot(a, b):
    return jnp.dot(a, b, preferred_element_type=jnp.float32)


def packed(edges, top, bottom):
    low = lax.broadcasted_iota(jnp.int32, top.shape, 1) < edges
    first = jnp.where(low, top, pltpu.roll(bottom, edges, 1))
    second = jnp.where(low, pltpu.roll(top, edges, 1), bottom)
    return first.astype(jnp.bfloat16), second.astype(jnp.bfloat16)


def project_block(pair, gain, weight_in, weight_gate):
    h = weight_in.shape[1] // 4
    w = weight_in[...]
    normed = layer_normalize(pair, gain[...]).astype(jnp.bfloat16)
    values = dot(normed, jnp.concatenate([w[:, :h], w[:, 2 * h : 3 * h]], axis=1))
    gates = dot(normed, jnp.concatenate([w[:, h : 2 * h], w[:, 3 * h :]], axis=1))
    return sigmoid(gates) * values, sigmoid(dot(normed, weight_gate[...]))


def finish_block(pair, gating, mixed, gain, weight_out):
    h = gain.shape[1]
    mixed = mixed.reshape(pair.shape)
    mixed = (mixed + pltpu.roll(mixed, h, 1))[:, :h]
    normed = layer_normalize(mixed, gain[...]).astype(jnp.bfloat16)
    update = dot(normed, weight_out[...])
    return (pair + gating * update).astype(jnp.bfloat16)


def kernel(
    samples,
    left_ref, right_ref, pair_ref, outer_w, outer_b,
    gain1, edge1, gate1, mid1, out1,
    gain2, edge2, gate2, mid2, out2,
    o_ref,
    lbuf, rbuf, psend, pbuf, y_scr,
    abuf, bsend, bbuf, a_scr, b_scr, mixed_scr,
    a2send, a2buf, b2buf, fsend, fbuf,
    send4, recv4, send16, recv16,
):
    me = lax.axis_index("res")
    z, m = me // 4, me % 4
    barrier = pltpu.get_barrier_semaphore()
    for d in range(1, 16):
        pl.semaphore_signal(
            barrier, inc=1, device_id={"res": (me + d) % 16}, device_id_type=pl.DeviceIdType.MESH
        )

    started = []

    def send(src, dst, ssem, rsem, target):
        copy = pltpu.make_async_remote_copy(
            src_ref=src, dst_ref=dst, send_sem=ssem, recv_sem=rsem,
            device_id={"res": target}, device_id_type=pl.DeviceIdType.MESH,
        )
        copy.start()
        started.append(copy)
        return copy

    def same_z(d):
        return z * 4 + (m + d) % 4

    def same_m(d):
        return ((z + d) % 4) * 4 + m

    to_blocks = selection(
        256, lambda r: field(r, 6, 3, 2) + field(r, 4, 3, 4) + field(r, 2, 3, 0) + field(r, 0, 3, 6)
    )
    psend[...] = dot(to_blocks, pair_ref[...]).astype(jnp.bfloat16).reshape(4, 64, 128)
    lbuf[m] = left_ref[...]
    rbuf[z] = right_ref[...]
    pbuf[m] = psend[m]

    pl.semaphore_wait(barrier, 15)
    r_copies = [
        send(right_ref, rbuf.at[z], send4.at[0, d], recv4.at[0, d], same_m(d)) for d in range(1, 4)
    ]
    l_copies = [
        send(left_ref, lbuf.at[m], send4.at[1, d], recv4.at[1, d], same_z(d)) for d in range(1, 4)
    ]
    p_copies = [
        send(psend.at[(m + d) % 4], pbuf.at[m], send4.at[2, d], recv4.at[2, d], same_z(d))
        for d in range(1, 4)
    ]
    order_left = selection(
        512, lambda r: field(r, 2, 3, 7) + field(r, 0, 3, 5) + field(r, 4, 7, 2) + field(r, 7, 3, 0)
    )
    for copy in l_copies:
        copy.wait_recv()
    left_t = sum(
        lax.dot_general(
            order_left[:, k * 128 : (k + 1) * 128], lbuf[k], (((1,), (1,)), ((), ())),
            preferred_element_type=jnp.float32,
        )
        for k in range(4)
    ).astype(jnp.bfloat16)
    for copy in p_copies:
        copy.wait_recv()
    order_pair = selection(
        256, lambda r: field(r, 2, 3, 6) + field(r, 6, 3, 4) + field(r, 4, 3, 2) + field(r, 0, 3, 0)
    )
    state = dot(order_pair, pbuf[...].reshape(256, 128))

    for copy in r_copies:
        copy.wait_recv()
    lane = lax.broadcasted_iota(jnp.int32, (128, 128), 1)
    for b in range(4):
        outer = dot(left_t, rbuf[b])
        x = [outer[k * 128 : (k + 1) * 128] for k in range(4)]
        low = lane < 64
        for u, v in ((0, 2), (1, 3)):
            x[u], x[v] = (
                jnp.where(low, x[u], pltpu.roll(x[v], 64, 1)),
                jnp.where(low, pltpu.roll(x[u], 64, 1), x[v]),
            )
        low = (lane & 32) == 0
        for u, v in ((0, 1), (2, 3)):
            x[u], x[v] = (
                jnp.where(low, x[u], pltpu.roll(x[v], 32, 1)),
                jnp.where(low, pltpu.roll(x[u], 96, 1), x[v]),
            )
        for k in range(4):
            y_scr[:, b * 4 + k] = (x[k] * (1.0 / samples)).astype(jnp.bfloat16).reshape(8, 16, 128)
    update = sum(
        dot(y_scr[a].reshape(256, 128), outer_w[a * 128 : (a + 1) * 128, :]) for a in range(8)
    )
    pair = (state + (update + outer_b[...])).astype(jnp.bfloat16).astype(jnp.float32)

    edges, gating = project_block(pair, gain1, edge1, gate1)
    a_half, b_half = packed(64, edges[:128], edges[128:])
    to_rows = selection(128, lambda r: field(r, 2, 7, 4) + field(r, 5, 3, 2) + field(r, 0, 3, 0))
    bsend[...] = dot(to_rows, b_half).astype(jnp.bfloat16).reshape(4, 32, 128)
    abuf[m] = a_half
    bbuf[z, m] = bsend[m]
    b_copies = [
        send(bsend.at[(me + d) % 4], bbuf.at[z, m], send16.at[0, d], recv16.at[0, d], (me + d) % 16)
        for d in range(1, 16)
    ]
    a_copies = [
        send(abuf.at[m], abuf.at[m], send4.at[3, d], recv4.at[3, d], same_z(d)) for d in range(1, 4)
    ]
    for copy in a_copies + b_copies:
        copy.wait_recv()
    a_scr[...] = abuf[...].astype(jnp.float32).reshape(32, 16, 128)
    b_scr[...] = bbuf[...].astype(jnp.float32)

    def outgoing(j, carry):
        zj, rj = j // 4, j % 4
        total = jnp.zeros((16, 128), jnp.float32)
        for k in range(32):
            total += a_scr[k] * b_scr[zj, k // 8, pl.ds((k % 8) * 4 + rj, 1), :]
        mixed_scr[j] = total
        return carry

    lax.fori_loop(0, 16, outgoing, 0)
    pair = finish_block(pair, gating, mixed_scr[...], mid1, out1).astype(jnp.float32)

    edges, gating = project_block(pair, gain2, edge2, gate2)
    halves = edges.reshape(16, 2, 8, 128)
    a_half, b_half = packed(64, halves[:, 0].reshape(128, 128), halves[:, 1].reshape(128, 128))
    a2send[...] = a_half.reshape(4, 32, 128)
    b2buf[z] = b_half
    a2buf[z, m] = a2send[z]
    b2_copies = [
        send(b2buf.at[z], b2buf.at[z], send4.at[4, d], recv4.at[4, d], same_m(d)) for d in range(1, 4)
    ]
    a2_copies = [
        send(
            a2send.at[((me + d) % 16) // 4], a2buf.at[z, m], send16.at[1, d], recv16.at[1, d],
            (me + d) % 16,
        )
        for d in range(1, 16)
    ]
    by_step = selection(128, lambda r: field(r, 2, 3, 5) + field(r, 0, 3, 3) + field(r, 4, 7, 0))
    for copy in a2_copies:
        copy.wait_recv()
    for k in range(4):
        a_scr[k * 8 : (k + 1) * 8] = dot(by_step, a2buf[k].reshape(128, 128)).reshape(8, 16, 128)
    for copy in b2_copies:
        copy.wait_recv()
    b_scr[...] = b2buf[...].astype(jnp.float32).reshape(b_scr.shape)

    def incoming(j, carry):
        jb, jr = j // 4, j % 4
        total = jnp.zeros((16, 128), jnp.float32)
        for k in range(32):
            total += a_scr[k] * b_scr[k // 8, jb, pl.ds(jr * 8 + k % 8, 1), :]
        mixed_scr[j] = total
        return carry

    lax.fori_loop(0, 16, incoming, 0)
    done = finish_block(pair, gating, mixed_scr[...], mid2, out2)

    from_blocks = selection(
        256, lambda r: field(r, 2, 3, 6) + field(r, 0, 3, 4) + field(r, 6, 3, 2) + field(r, 4, 3, 0)
    )
    fsend[...] = dot(from_blocks, done).astype(jnp.bfloat16).reshape(4, 64, 128)
    fbuf[m] = fsend[m]
    f_copies = [
        send(fsend.at[(m + d) % 4], fbuf.at[m], send4.at[5, d], recv4.at[5, d], same_z(d))
        for d in range(1, 4)
    ]
    for copy in f_copies:
        copy.wait_recv()
    o_ref[...] = fbuf[...]
    for copy in started:
        copy.wait_send()


def blocks(*args):
    embedding, pair_state, norm_scale, former, latter = args[:5]
    samples, rows, channels = embedding.shape
    normed = layer_normalize(embedding.astype(jnp.float32), norm_scale).astype(jnp.bfloat16)
    left, right = (
        jnp.einsum("vfd,dl->vfl", normed, w, preferred_element_type=jnp.float32)
        .astype(jnp.bfloat16)
        .reshape(samples, -1)
        for w in (former, latter)
    )
    rest = [a.reshape(1, -1) if a.ndim == 1 else a for a in args[5:]]
    bf16, f32 = jnp.bfloat16, jnp.float32
    vmem = pl.BlockSpec(memory_space=pltpu.VMEM)
    out = pl.pallas_call(
        functools.partial(kernel, samples),
        out_shape=jax.ShapeDtypeStruct((4, 64, 128), bf16),
        in_specs=[vmem] * (3 + len(rest)),
        out_specs=vmem,
        scratch_shapes=[
            pltpu.VMEM((4, 256, 128), bf16),
            pltpu.VMEM((4, 256, 128), bf16),
            pltpu.VMEM((4, 64, 128), bf16),
            pltpu.VMEM((4, 64, 128), bf16),
            pltpu.VMEM((8, 16, 16, 128), bf16),
            pltpu.VMEM((4, 128, 128), bf16),
            pltpu.VMEM((4, 32, 128), bf16),
            pltpu.VMEM((4, 4, 32, 128), bf16),
            pltpu.VMEM((32, 16, 128), f32),
            pltpu.VMEM((4, 4, 32, 128), f32),
            pltpu.VMEM((16, 16, 128), f32),
            pltpu.VMEM((4, 32, 128), bf16),
            pltpu.VMEM((4, 4, 32, 128), bf16),
            pltpu.VMEM((4, 128, 128), bf16),
            pltpu.VMEM((4, 64, 128), bf16),
            pltpu.VMEM((4, 64, 128), bf16),
            pltpu.SemaphoreType.DMA((6, 4)),
            pltpu.SemaphoreType.DMA((6, 4)),
            pltpu.SemaphoreType.DMA((2, 16)),
            pltpu.SemaphoreType.DMA((2, 16)),
        ],
        compiler_params=pltpu.CompilerParams(
            collective_id=0, has_side_effects=True, vmem_limit_bytes=32 * 1024 * 1024
        ),
    )(left, right, pair_state.reshape(256, 128), *rest)
    return out.reshape(4, 4, 4, 4, 128).transpose(1, 2, 0, 3, 4).reshape(pair_state.shape)


def fits_blocks(mesh, embedding, pair_state, former, edge_weight):
    return (
        mesh.shape["res"] == 16
        and pair_state.shape[1:] == (64, 128)
        and embedding.shape[0] // mesh.shape["groups"] == 256
        and former.shape[1] == 32
        and edge_weight.shape == (128, 256)
    )


def solution(mesh):
    in_specs = (
        P("groups", "res", None),
        P(("groups", "res"), None, None),
        P(),
        P(),
        P(),
        P(),
        P(),
        P(),
        P(),
        P(),
        P(),
        P(),
        P(),
        P(),
        P(),
        P(),
        P(),
    )
    out_specs = P(("groups", "res"), None, None)

    def program(*args):
        blocked = fits_blocks(mesh, args[0], args[1], args[3], args[8])
        return jax.shard_map(
            blocks if blocked else shards,
            mesh=mesh, in_specs=in_specs, out_specs=out_specs, check_vma=False,
        )(*args)

    return program
```

```python
import functools

import jax
import jax.numpy as jnp
from jax import lax
from jax.experimental import pallas as pl
from jax.experimental.pallas import tpu as pltpu
from jax.sharding import PartitionSpec as P


def layer_normalize(values, gain):
    mean_val = jnp.mean(values, axis=-1, keepdims=True)
    centred = values - mean_val
    variance = jnp.mean(centred * centred, axis=-1, keepdims=True)
    return centred / jnp.sqrt(variance + 1e-05) * gain


def project_in(pair_block, norm_gain, weight_in, weight_gate):
    hidden_width = weight_in.shape[1] // 4
    normed = layer_normalize(pair_block.astype(jnp.float32), norm_gain).astype(jnp.bfloat16)
    projected = jnp.einsum("abc,cd->abd", normed, weight_in, preferred_element_type=jnp.float32)
    edge_left = (
        jax.nn.sigmoid(projected[..., hidden_width : 2 * hidden_width])
        * projected[..., :hidden_width]
    ).astype(jnp.bfloat16)
    edge_right = (
        jax.nn.sigmoid(projected[..., 3 * hidden_width :])
        * projected[..., 2 * hidden_width : 3 * hidden_width]
    ).astype(jnp.bfloat16)
    gating = jax.nn.sigmoid(
        jnp.einsum("abc,cd->abd", normed, weight_gate, preferred_element_type=jnp.float32)
    )
    return (edge_left, edge_right, gating)


def apply_update(pair_block, gating, mixed_normed, weight_final):
    update = jnp.einsum(
        "abc,cd->abd", mixed_normed, weight_final, preferred_element_type=jnp.float32
    )
    return (pair_block.astype(jnp.float32) + gating * update).astype(jnp.bfloat16)


def shards(
    homolog_embedding,
    pair_state,
    homolog_norm_scale,
    former_operand_matrix,
    latter_operand_matrix,
    outer_mean_weight,
    outer_mean_bias,
    outgoing_input_gain,
    outgoing_edge_weight,
    outgoing_gate_weight,
    outgoing_product_gain,
    outgoing_output_weight,
    incoming_input_gain,
    incoming_edge_weight,
    incoming_gate_weight,
    incoming_product_gain,
    incoming_output_weight,
):
    sequence_rows = homolog_embedding.shape[0]
    alignment_normalized = layer_normalize(
        homolog_embedding.astype(jnp.float32), homolog_norm_scale
    ).astype(jnp.bfloat16)
    left_factor = jnp.einsum(
        "vfd,dl->vfl",
        alignment_normalized,
        former_operand_matrix,
        preferred_element_type=jnp.float32,
    ).astype(jnp.bfloat16)
    right_factor = jnp.einsum(
        "vfd,dl->vfl",
        alignment_normalized,
        latter_operand_matrix,
        preferred_element_type=jnp.float32,
    ).astype(jnp.bfloat16)
    outer = (
        jnp.einsum(
            "sip,sjq->ijpq",
            left_factor,
            lax.all_gather(right_factor, "res", axis=1, tiled=True),
            preferred_element_type=jnp.float32,
        )
        / sequence_rows
    )
    flattened = outer.reshape(outer.shape[0], outer.shape[1], -1).astype(jnp.bfloat16)
    outer_update = (
        jnp.einsum("ijr,rc->ijc", flattened, outer_mean_weight, preferred_element_type=jnp.float32)
        + outer_mean_bias
    )
    pair_one = (pair_state.astype(jnp.float32) + outer_update).astype(jnp.bfloat16)
    edge_left, edge_right, gating = project_in(
        pair_one, outgoing_input_gain, outgoing_edge_weight, outgoing_gate_weight
    )
    mixed = jnp.einsum(
        "ikc,jkc->ijc",
        edge_left,
        lax.all_gather(edge_right, "res", axis=0, tiled=True),
        preferred_element_type=jnp.float32,
    )
    mixed_normed = layer_normalize(mixed, outgoing_product_gain).astype(jnp.bfloat16)
    pair_two = apply_update(pair_one, gating, mixed_normed, outgoing_output_weight)
    in_left, in_right, in_gating = project_in(
        pair_two, incoming_input_gain, incoming_edge_weight, incoming_gate_weight
    )
    in_mixed = jnp.einsum(
        "kic,kjc->ijc",
        lax.all_to_all(in_left, "res", split_axis=1, concat_axis=0, tiled=True),
        lax.all_gather(in_right, "res", axis=0, tiled=True),
        preferred_element_type=jnp.float32,
    )
    in_normed = layer_normalize(in_mixed, incoming_product_gain).astype(jnp.bfloat16)
    return apply_update(pair_two, in_gating, in_normed, incoming_output_weight)


def sigmoid(values):
    return 1.0 / (1.0 + jnp.exp(-values))


def selection(size, source_row):
    out_row = lax.broadcasted_iota(jnp.int32, (size, size), 0)
    column = lax.broadcasted_iota(jnp.int32, (size, size), 1)
    return jnp.where(source_row(out_row) == column, 1.0, 0.0).astype(jnp.bfloat16)


def field(value, low, mask, to):
    return ((value >> low) & mask) << to


def dot(a, b):
    return jnp.dot(a, b, preferred_element_type=jnp.float32)


def packed(edges, top, bottom):
    low = lax.broadcasted_iota(jnp.int32, top.shape, 1) < edges
    first = jnp.where(low, top, pltpu.roll(bottom, edges, 1))
    second = jnp.where(low, pltpu.roll(top, edges, 1), bottom)
    return first.astype(jnp.bfloat16), second.astype(jnp.bfloat16)


def project_block(pair, gain, weight_in, weight_gate):
    h = weight_in.shape[1] // 4
    w = weight_in[...]
    normed = layer_normalize(pair, gain[...]).astype(jnp.bfloat16)
    values = dot(normed, jnp.concatenate([w[:, :h], w[:, 2 * h : 3 * h]], axis=1))
    gates = dot(normed, jnp.concatenate([w[:, h : 2 * h], w[:, 3 * h :]], axis=1))
    return sigmoid(gates) * values, sigmoid(dot(normed, weight_gate[...]))


def finish_block(pair, gating, mixed, gain, weight_out):
    h = gain.shape[1]
    mixed = mixed.reshape(pair.shape)
    mixed = (mixed + pltpu.roll(mixed, h, 1))[:, :h]
    normed = layer_normalize(mixed, gain[...]).astype(jnp.bfloat16)
    update = dot(normed, weight_out[...])
    return (pair + gating * update).astype(jnp.bfloat16)


def kernel(
    samples,
    msa_ref, msa_gain, former, latter, pair_ref, outer_w, outer_b,
    gain1, edge1, gate1, mid1, out1,
    gain2, edge2, gate2, mid2, out2,
    o_ref,
    msa_scr, lbuf, rbuf, psend, pbuf, y_scr,
    abuf, bsend, bbuf, a_scr, b_scr, mixed_scr,
    a2send, a2buf, b2buf, fsend, fbuf,
    send4, recv4, send16, recv16,
):
    me = lax.axis_index("res")
    z, m = me // 4, me % 4
    barrier = pltpu.get_barrier_semaphore()
    for d in range(1, 16):
        pl.semaphore_signal(
            barrier, inc=1, device_id={"res": (me + d) % 16}, device_id_type=pl.DeviceIdType.MESH
        )

    started = []

    def send(src, dst, ssem, rsem, target):
        copy = pltpu.make_async_remote_copy(
            src_ref=src, dst_ref=dst, send_sem=ssem, recv_sem=rsem,
            device_id={"res": target}, device_id_type=pl.DeviceIdType.MESH,
        )
        copy.start()
        started.append(copy)
        return copy

    def same_z(d):
        return z * 4 + (m + d) % 4

    def same_m(d):
        return ((z + d) % 4) * 4 + m

    to_blocks = selection(
        256, lambda r: field(r, 6, 3, 2) + field(r, 4, 3, 4) + field(r, 2, 3, 0) + field(r, 0, 3, 6)
    )
    psend[...] = dot(to_blocks, pair_ref[...]).astype(jnp.bfloat16).reshape(4, 64, 128)
    pbuf[m] = psend[m]

    msa_scr[...] = msa_ref[...].astype(jnp.float32)
    weights = jnp.concatenate([former[...]] * 4 + [latter[...]] * 4, axis=1)
    position = (lax.broadcasted_iota(jnp.int32, weights.shape, 1) >> 5) & 3
    factors = jnp.zeros((msa_ref.shape[0], 256), jnp.float32)
    for r in range(4):
        normed = layer_normalize(msa_scr[:, r, :], msa_gain[...]).astype(jnp.bfloat16)
        own = jnp.where(position == r, weights.astype(jnp.float32), 0.0).astype(jnp.bfloat16)
        factors += dot(normed, own)
    lbuf[m] = factors[:, :128].astype(jnp.bfloat16)
    rbuf[z] = factors[:, 128:].astype(jnp.bfloat16)

    pl.semaphore_wait(barrier, 15)
    _ = [
        send(rbuf.at[z], rbuf.at[z], send4.at[0, d], recv4.at[0, z], same_m(d)) for d in range(1, 4)
    ]
    l_copies = [
        send(lbuf.at[m], lbuf.at[m], send4.at[1, d], recv4.at[1, d], same_z(d)) for d in range(1, 4)
    ]
    p_copies = [
        send(psend.at[(m + d) % 4], pbuf.at[m], send4.at[2, d], recv4.at[2, d], same_z(d))
        for d in range(1, 4)
    ]
    order_left = selection(
        512, lambda r: field(r, 2, 3, 7) + field(r, 0, 3, 5) + field(r, 4, 7, 2) + field(r, 7, 3, 0)
    )
    for copy in l_copies:
        copy.wait_recv()
    left_t = sum(
        lax.dot_general(
            order_left[:, k * 128 : (k + 1) * 128], lbuf[k], (((1,), (1,)), ((), ())),
            preferred_element_type=jnp.float32,
        )
        for k in range(4)
    ).astype(jnp.bfloat16)
    for copy in p_copies:
        copy.wait_recv()
    order_pair = selection(
        256, lambda r: field(r, 2, 3, 6) + field(r, 6, 3, 4) + field(r, 4, 3, 2) + field(r, 0, 3, 0)
    )
    state = dot(order_pair, pbuf[...].reshape(256, 128))

    near = jnp.where(z == 0, 1, z - 1)
    middle = jnp.where(z == 0, 2, jnp.where(z == 3, 1, z + 1))
    lane = lax.broadcasted_iota(jnp.int32, (128, 128), 1)
    for b in (z, near, middle, 6 - z - near - middle):
        if b is not z:
            pltpu.make_async_remote_copy(
                src_ref=rbuf.at[z], dst_ref=rbuf.at[b], send_sem=send4.at[0, 0],
                recv_sem=recv4.at[0, b], device_id={"res": b * 4 + m},
                device_id_type=pl.DeviceIdType.MESH,
            ).wait_recv()
        outer = dot(left_t, rbuf[b])
        x = [outer[k * 128 : (k + 1) * 128] for k in range(4)]
        low = lane < 64
        for u, v in ((0, 2), (1, 3)):
            x[u], x[v] = (
                jnp.where(low, x[u], pltpu.roll(x[v], 64, 1)),
                jnp.where(low, pltpu.roll(x[u], 64, 1), x[v]),
            )
        low = (lane & 32) == 0
        for u, v in ((0, 1), (2, 3)):
            x[u], x[v] = (
                jnp.where(low, x[u], pltpu.roll(x[v], 32, 1)),
                jnp.where(low, pltpu.roll(x[u], 96, 1), x[v]),
            )
        for k in range(4):
            y_scr[:, b * 4 + k] = (x[k] * (1.0 / samples)).astype(jnp.bfloat16).reshape(8, 16, 128)
    update = sum(
        dot(y_scr[a].reshape(256, 128), outer_w[a * 128 : (a + 1) * 128, :]) for a in range(8)
    )
    pair = (state + (update + outer_b[...])).astype(jnp.bfloat16).astype(jnp.float32)

    edges, gating = project_block(pair, gain1, edge1, gate1)
    a_half, b_half = packed(64, edges[:128], edges[128:])
    to_rows = selection(128, lambda r: field(r, 2, 7, 4) + field(r, 5, 3, 2) + field(r, 0, 3, 0))
    bsend[...] = dot(to_rows, b_half).astype(jnp.bfloat16).reshape(4, 32, 128)
    abuf[m] = a_half
    bbuf[z, m] = bsend[m]
    b_copies = [
        send(bsend.at[(me + d) % 4], bbuf.at[z, m], send16.at[0, d], recv16.at[0, d], (me + d) % 16)
        for d in range(1, 16)
    ]
    a_copies = [
        send(abuf.at[m], abuf.at[m], send4.at[3, d], recv4.at[3, d], same_z(d)) for d in range(1, 4)
    ]
    for copy in a_copies + b_copies:
        copy.wait_recv()
    a_scr[...] = abuf[...].astype(jnp.float32).reshape(32, 16, 128)
    b_scr[...] = bbuf[...].astype(jnp.float32)

    def outgoing(j, carry):
        zj, rj = j // 4, j % 4
        total = jnp.zeros((16, 128), jnp.float32)
        for k in range(32):
            total += a_scr[k] * b_scr[zj, k // 8, pl.ds((k % 8) * 4 + rj, 1), :]
        mixed_scr[j] = total
        return carry

    lax.fori_loop(0, 16, outgoing, 0, unroll=4)
    pair = finish_block(pair, gating, mixed_scr[...], mid1, out1).astype(jnp.float32)

    edges, gating = project_block(pair, gain2, edge2, gate2)
    halves = edges.reshape(16, 2, 8, 128)
    a_half, b_half = packed(64, halves[:, 0].reshape(128, 128), halves[:, 1].reshape(128, 128))
    a2send[...] = a_half.reshape(4, 32, 128)
    b2buf[z] = b_half
    a2buf[z, m] = a2send[z]
    a2_copies = [
        send(
            a2send.at[((me + d) % 16) // 4], a2buf.at[z, m], send16.at[1, d], recv16.at[1, d],
            (me + d) % 16,
        )
        for d in range(1, 16)
    ]
    b2_copies = [
        send(b2buf.at[z], b2buf.at[z], send4.at[4, d], recv4.at[4, d], same_m(d)) for d in range(1, 4)
    ]
    by_step = selection(128, lambda r: field(r, 2, 3, 5) + field(r, 0, 3, 3) + field(r, 4, 7, 0))
    for copy in a2_copies:
        copy.wait_recv()
    for k in range(4):
        a_scr[k * 8 : (k + 1) * 8] = dot(by_step, a2buf[k].reshape(128, 128)).reshape(8, 16, 128)
    for copy in b2_copies:
        copy.wait_recv()
    b_scr[...] = b2buf[...].astype(jnp.float32).reshape(b_scr.shape)

    def incoming(j, carry):
        jb, jr = j // 4, j % 4
        total = jnp.zeros((16, 128), jnp.float32)
        for k in range(32):
            total += a_scr[k] * b_scr[k // 8, jb, pl.ds(jr * 8 + k % 8, 1), :]
        mixed_scr[j] = total
        return carry

    lax.fori_loop(0, 16, incoming, 0, unroll=4)
    done = finish_block(pair, gating, mixed_scr[...], mid2, out2)

    from_blocks = selection(
        256, lambda r: field(r, 2, 3, 6) + field(r, 0, 3, 4) + field(r, 6, 3, 2) + field(r, 4, 3, 0)
    )
    fsend[...] = dot(from_blocks, done).astype(jnp.bfloat16).reshape(4, 64, 128)
    fbuf[m] = fsend[m]
    f_copies = [
        send(fsend.at[(m + d) % 4], fbuf.at[m], send4.at[5, d], recv4.at[5, d], same_z(d))
        for d in range(1, 4)
    ]
    for copy in f_copies:
        copy.wait_recv()
    o_ref[...] = fbuf[...]
    for copy in started:
        copy.wait_send()


def blocks(*args):
    embedding, pair_state, norm_scale, former, latter = args[:5]
    samples = embedding.shape[0]
    rest = [a.reshape(1, -1) if a.ndim == 1 else a for a in args[5:]]
    bf16, f32 = jnp.bfloat16, jnp.float32
    vmem = pl.BlockSpec(memory_space=pltpu.VMEM)
    out = pl.pallas_call(
        functools.partial(kernel, samples),
        out_shape=jax.ShapeDtypeStruct((4, 64, 128), bf16),
        in_specs=[vmem] * (5 + len(rest)),
        out_specs=vmem,
        scratch_shapes=[
            pltpu.VMEM(embedding.shape, f32),
            pltpu.VMEM((4, 256, 128), bf16),
            pltpu.VMEM((4, 256, 128), bf16),
            pltpu.VMEM((4, 64, 128), bf16),
            pltpu.VMEM((4, 64, 128), bf16),
            pltpu.VMEM((8, 16, 16, 128), bf16),
            pltpu.VMEM((4, 128, 128), bf16),
            pltpu.VMEM((4, 32, 128), bf16),
            pltpu.VMEM((4, 4, 32, 128), bf16),
            pltpu.VMEM((32, 16, 128), f32),
            pltpu.VMEM((4, 4, 32, 128), f32),
            pltpu.VMEM((16, 16, 128), f32),
            pltpu.VMEM((4, 32, 128), bf16),
            pltpu.VMEM((4, 4, 32, 128), bf16),
            pltpu.VMEM((4, 128, 128), bf16),
            pltpu.VMEM((4, 64, 128), bf16),
            pltpu.VMEM((4, 64, 128), bf16),
            pltpu.SemaphoreType.DMA((6, 4)),
            pltpu.SemaphoreType.DMA((6, 4)),
            pltpu.SemaphoreType.DMA((2, 16)),
            pltpu.SemaphoreType.DMA((2, 16)),
        ],
        compiler_params=pltpu.CompilerParams(
            collective_id=0, has_side_effects=True, vmem_limit_bytes=32 * 1024 * 1024
        ),
    )(embedding, norm_scale.reshape(1, -1), former, latter, pair_state.reshape(256, 128), *rest)
    return out.reshape(4, 4, 4, 4, 128).transpose(1, 2, 0, 3, 4).reshape(pair_state.shape)


def fits_blocks(mesh, embedding, pair_state, former, edge_weight):
    return (
        mesh.shape["res"] == 16
        and pair_state.shape[1:] == (64, 128)
        and embedding.shape[0] // mesh.shape["groups"] == 256
        and former.shape[1] == 32
        and edge_weight.shape == (128, 256)
    )


def solution(mesh):
    in_specs = (
        P("groups", "res", None),
        P(("groups", "res"), None, None),
        P(),
        P(),
        P(),
        P(),
        P(),
        P(),
        P(),
        P(),
        P(),
        P(),
        P(),
        P(),
        P(),
        P(),
        P(),
    )
    out_specs = P(("groups", "res"), None, None)

    def program(*args):
        blocked = fits_blocks(mesh, args[0], args[1], args[3], args[8])
        return jax.shard_map(
            blocks if blocked else shards,
            mesh=mesh, in_specs=in_specs, out_specs=out_specs, check_vma=False,
        )(*args)

    return program
```

```python
import functools

import jax
import jax.numpy as jnp
from jax import lax
from jax.experimental import pallas as pl
from jax.experimental.pallas import tpu as pltpu
from jax.sharding import PartitionSpec as P


def layer_normalize(values, gain):
    mean_val = jnp.mean(values, axis=-1, keepdims=True)
    centred = values - mean_val
    variance = jnp.mean(centred * centred, axis=-1, keepdims=True)
    return centred / jnp.sqrt(variance + 1e-05) * gain


def project_in(pair_block, norm_gain, weight_in, weight_gate):
    hidden_width = weight_in.shape[1] // 4
    normed = layer_normalize(pair_block.astype(jnp.float32), norm_gain).astype(jnp.bfloat16)
    projected = jnp.einsum("abc,cd->abd", normed, weight_in, preferred_element_type=jnp.float32)
    edge_left = (
        jax.nn.sigmoid(projected[..., hidden_width : 2 * hidden_width])
        * projected[..., :hidden_width]
    ).astype(jnp.bfloat16)
    edge_right = (
        jax.nn.sigmoid(projected[..., 3 * hidden_width :])
        * projected[..., 2 * hidden_width : 3 * hidden_width]
    ).astype(jnp.bfloat16)
    gating = jax.nn.sigmoid(
        jnp.einsum("abc,cd->abd", normed, weight_gate, preferred_element_type=jnp.float32)
    )
    return (edge_left, edge_right, gating)


def apply_update(pair_block, gating, mixed_normed, weight_final):
    update = jnp.einsum(
        "abc,cd->abd", mixed_normed, weight_final, preferred_element_type=jnp.float32
    )
    return (pair_block.astype(jnp.float32) + gating * update).astype(jnp.bfloat16)


def shards(
    homolog_embedding,
    pair_state,
    homolog_norm_scale,
    former_operand_matrix,
    latter_operand_matrix,
    outer_mean_weight,
    outer_mean_bias,
    outgoing_input_gain,
    outgoing_edge_weight,
    outgoing_gate_weight,
    outgoing_product_gain,
    outgoing_output_weight,
    incoming_input_gain,
    incoming_edge_weight,
    incoming_gate_weight,
    incoming_product_gain,
    incoming_output_weight,
):
    sequence_rows = homolog_embedding.shape[0]
    alignment_normalized = layer_normalize(
        homolog_embedding.astype(jnp.float32), homolog_norm_scale
    ).astype(jnp.bfloat16)
    left_factor = jnp.einsum(
        "vfd,dl->vfl",
        alignment_normalized,
        former_operand_matrix,
        preferred_element_type=jnp.float32,
    ).astype(jnp.bfloat16)
    right_factor = jnp.einsum(
        "vfd,dl->vfl",
        alignment_normalized,
        latter_operand_matrix,
        preferred_element_type=jnp.float32,
    ).astype(jnp.bfloat16)
    outer = (
        jnp.einsum(
            "sip,sjq->ijpq",
            left_factor,
            lax.all_gather(right_factor, "res", axis=1, tiled=True),
            preferred_element_type=jnp.float32,
        )
        / sequence_rows
    )
    flattened = outer.reshape(outer.shape[0], outer.shape[1], -1).astype(jnp.bfloat16)
    outer_update = (
        jnp.einsum("ijr,rc->ijc", flattened, outer_mean_weight, preferred_element_type=jnp.float32)
        + outer_mean_bias
    )
    pair_one = (pair_state.astype(jnp.float32) + outer_update).astype(jnp.bfloat16)
    edge_left, edge_right, gating = project_in(
        pair_one, outgoing_input_gain, outgoing_edge_weight, outgoing_gate_weight
    )
    mixed = jnp.einsum(
        "ikc,jkc->ijc",
        edge_left,
        lax.all_gather(edge_right, "res", axis=0, tiled=True),
        preferred_element_type=jnp.float32,
    )
    mixed_normed = layer_normalize(mixed, outgoing_product_gain).astype(jnp.bfloat16)
    pair_two = apply_update(pair_one, gating, mixed_normed, outgoing_output_weight)
    in_left, in_right, in_gating = project_in(
        pair_two, incoming_input_gain, incoming_edge_weight, incoming_gate_weight
    )
    in_mixed = jnp.einsum(
        "kic,kjc->ijc",
        lax.all_to_all(in_left, "res", split_axis=1, concat_axis=0, tiled=True),
        lax.all_gather(in_right, "res", axis=0, tiled=True),
        preferred_element_type=jnp.float32,
    )
    in_normed = layer_normalize(in_mixed, incoming_product_gain).astype(jnp.bfloat16)
    return apply_update(pair_two, in_gating, in_normed, incoming_output_weight)


def sigmoid(values):
    return 1.0 / (1.0 + jnp.exp(-values))


def selection(size, source_row):
    out_row = lax.broadcasted_iota(jnp.int32, (size, size), 0)
    column = lax.broadcasted_iota(jnp.int32, (size, size), 1)
    return jnp.where(source_row(out_row) == column, 1.0, 0.0).astype(jnp.bfloat16)


def field(value, low, mask, to):
    return ((value >> low) & mask) << to


def dot(a, b):
    return jnp.dot(a, b, preferred_element_type=jnp.float32)


def packed(edges, top, bottom):
    low = lax.broadcasted_iota(jnp.int32, top.shape, 1) < edges
    first = jnp.where(low, top, pltpu.roll(bottom, edges, 1))
    second = jnp.where(low, pltpu.roll(top, edges, 1), bottom)
    return first.astype(jnp.bfloat16), second.astype(jnp.bfloat16)


def project_block(pair, gain, weight_in, weight_gate):
    h = weight_in.shape[1] // 4
    w = weight_in[...]
    normed = layer_normalize(pair, gain[...]).astype(jnp.bfloat16)
    values = dot(normed, jnp.concatenate([w[:, :h], w[:, 2 * h : 3 * h]], axis=1))
    gates = dot(normed, jnp.concatenate([w[:, h : 2 * h], w[:, 3 * h :]], axis=1))
    return sigmoid(gates) * values, sigmoid(dot(normed, weight_gate[...]))


def finish_block(pair, gating, mixed, gain, weight_out):
    h = gain.shape[1]
    mixed = mixed.reshape(pair.shape)
    mixed = (mixed + pltpu.roll(mixed, h, 1))[:, :h]
    normed = layer_normalize(mixed, gain[...]).astype(jnp.bfloat16)
    update = dot(normed, weight_out[...])
    return (pair + gating * update).astype(jnp.bfloat16)


def kernel(samples, *refs):
    count = (len(refs) - 23) // 2
    operands, o_ref, held, scratch = (
        refs[:count], refs[count], refs[count + 1 : 2 * count + 1], refs[2 * count + 1 :]
    )
    load_sem = scratch[-1]
    loads = [
        pltpu.make_async_copy(operand, here, load_sem.at[k])
        for k, (operand, here) in enumerate(zip(operands, held))
    ]
    for load in loads:
        load.start()
    body(samples, loads, *held, o_ref, *scratch[:-1])


def body(
    samples, loads,
    msa_ref, msa_gain, former, latter, pair_ref, outer_w, outer_b,
    gain1, edge1, gate1, mid1, out1,
    gain2, edge2, gate2, mid2, out2,
    o_ref,
    msa_scr, lbuf, rbuf, psend, pbuf, y_scr,
    abuf, bsend, bbuf, a_scr, b_scr, mixed_scr,
    a2send, a2buf, b2buf, fsend, fbuf,
    send4, recv4, send16, recv16,
):
    me = lax.axis_index("res")
    z, m = me // 4, me % 4
    barrier = pltpu.get_barrier_semaphore()
    for d in range(1, 16):
        pl.semaphore_signal(
            barrier, inc=1, device_id={"res": (me + d) % 16}, device_id_type=pl.DeviceIdType.MESH
        )

    started = []

    def send(src, dst, ssem, rsem, target):
        copy = pltpu.make_async_remote_copy(
            src_ref=src, dst_ref=dst, send_sem=ssem, recv_sem=rsem,
            device_id={"res": target}, device_id_type=pl.DeviceIdType.MESH,
        )
        copy.start()
        started.append(copy)
        return copy

    def same_z(d):
        return z * 4 + (m + d) % 4

    def same_m(d):
        return ((z + d) % 4) * 4 + m

    to_blocks = selection(
        256, lambda r: field(r, 6, 3, 2) + field(r, 4, 3, 4) + field(r, 2, 3, 0) + field(r, 0, 3, 6)
    )
    loads[4].wait()
    psend[...] = dot(to_blocks, pair_ref[...]).astype(jnp.bfloat16).reshape(4, 64, 128)
    pbuf[m] = psend[m]

    for load in loads[:4]:
        load.wait()
    msa_scr[...] = msa_ref[...].astype(jnp.float32)
    weights = jnp.concatenate([former[...]] * 4 + [latter[...]] * 4, axis=0)
    position = (lax.broadcasted_iota(jnp.int32, weights.shape, 0) >> 5) & 3
    factors = jnp.zeros((msa_ref.shape[0], 256), jnp.float32)
    for r in range(4):
        normed = layer_normalize(msa_scr[:, r, :], msa_gain[...]).astype(jnp.bfloat16)
        own = jnp.where(position == r, weights.astype(jnp.float32), 0.0).astype(jnp.bfloat16)
        factors += lax.dot_general(
            normed, own, (((1,), (1,)), ((), ())), preferred_element_type=jnp.float32
        )
    lbuf[m] = factors[:, :128].astype(jnp.bfloat16)
    rbuf[z] = factors[:, 128:].astype(jnp.bfloat16)

    pl.semaphore_wait(barrier, 15)
    for d in range(1, 4):
        send(rbuf.at[z], rbuf.at[z], send4.at[0, d], recv4.at[0, z], same_m(d))
    l_copies = [
        send(lbuf.at[m], lbuf.at[m], send4.at[1, d], recv4.at[1, d], same_z(d)) for d in range(1, 4)
    ]
    p_copies = [
        send(psend.at[(m + d) % 4], pbuf.at[m], send4.at[2, d], recv4.at[2, d], same_z(d))
        for d in range(1, 4)
    ]
    order_left = selection(
        512, lambda r: field(r, 2, 3, 7) + field(r, 0, 3, 5) + field(r, 4, 7, 2) + field(r, 7, 3, 0)
    )
    for copy in l_copies:
        copy.wait_recv()
    left_t = sum(
        lax.dot_general(
            order_left[:, k * 128 : (k + 1) * 128], lbuf[k], (((1,), (1,)), ((), ())),
            preferred_element_type=jnp.float32,
        )
        for k in range(4)
    ).astype(jnp.bfloat16)
    for copy in p_copies:
        copy.wait_recv()
    order_pair = selection(
        256, lambda r: field(r, 2, 3, 6) + field(r, 6, 3, 4) + field(r, 4, 3, 2) + field(r, 0, 3, 0)
    )
    state = dot(order_pair, pbuf[...].reshape(256, 128))

    near = jnp.where(z == 0, 1, z - 1)
    middle = jnp.where(z == 0, 2, jnp.where(z == 3, 1, z + 1))
    lane = lax.broadcasted_iota(jnp.int32, (128, 128), 1)
    for b in (z, near, middle, 6 - z - near - middle):
        if b is not z:
            pltpu.make_async_remote_copy(
                src_ref=rbuf.at[z], dst_ref=rbuf.at[b], send_sem=send4.at[0, 0],
                recv_sem=recv4.at[0, b], device_id={"res": b * 4 + m},
                device_id_type=pl.DeviceIdType.MESH,
            ).wait_recv()
        outer = dot(left_t, rbuf[b])
        x = [outer[k * 128 : (k + 1) * 128] for k in range(4)]
        low = lane < 64
        for u, v in ((0, 2), (1, 3)):
            x[u], x[v] = (
                jnp.where(low, x[u], pltpu.roll(x[v], 64, 1)),
                jnp.where(low, pltpu.roll(x[u], 64, 1), x[v]),
            )
        low = (lane & 32) == 0
        for u, v in ((0, 1), (2, 3)):
            x[u], x[v] = (
                jnp.where(low, x[u], pltpu.roll(x[v], 32, 1)),
                jnp.where(low, pltpu.roll(x[u], 96, 1), x[v]),
            )
        for k in range(4):
            y_scr[:, b * 4 + k] = (x[k] * (1.0 / samples)).astype(jnp.bfloat16).reshape(8, 16, 128)
    for load in loads[5:]:
        load.wait()
    update = sum(
        dot(y_scr[a].reshape(256, 128), outer_w[a * 128 : (a + 1) * 128, :]) for a in range(8)
    )
    pair = (state + (update + outer_b[...])).astype(jnp.bfloat16).astype(jnp.float32)

    edges, gating = project_block(pair, gain1, edge1, gate1)
    a_half, b_half = packed(64, edges[:128], edges[128:])
    to_rows = selection(128, lambda r: field(r, 2, 7, 4) + field(r, 5, 3, 2) + field(r, 0, 3, 0))
    bsend[...] = dot(to_rows, b_half).astype(jnp.bfloat16).reshape(4, 32, 128)
    abuf[m] = a_half
    bbuf[z, m] = bsend[m]
    b_copies = [
        send(bsend.at[(me + d) % 4], bbuf.at[z, m], send16.at[0, d], recv16.at[0, d], (me + d) % 16)
        for d in range(1, 16)
    ]
    a_copies = [
        send(abuf.at[m], abuf.at[m], send4.at[3, d], recv4.at[3, d], same_z(d)) for d in range(1, 4)
    ]
    for copy in a_copies + b_copies:
        copy.wait_recv()
    a_scr[...] = abuf[...].astype(jnp.float32).reshape(32, 16, 128)
    b_scr[...] = bbuf[...].astype(jnp.float32)

    def outgoing(j, carry):
        zj, rj = j // 4, j % 4
        parts = [jnp.zeros((16, 128), jnp.float32) for _ in range(4)]
        for k in range(32):
            parts[k % 4] += a_scr[k] * b_scr[zj, k // 8, pl.ds((k % 8) * 4 + rj, 1), :]
        mixed_scr[j] = (parts[0] + parts[1]) + (parts[2] + parts[3])
        return carry

    lax.fori_loop(0, 16, outgoing, 0, unroll=4)
    pair = finish_block(pair, gating, mixed_scr[...], mid1, out1).astype(jnp.float32)

    edges, gating = project_block(pair, gain2, edge2, gate2)
    halves = edges.reshape(16, 2, 8, 128)
    a_half, b_half = packed(64, halves[:, 0].reshape(128, 128), halves[:, 1].reshape(128, 128))
    a2send[...] = a_half.reshape(4, 32, 128)
    b2buf[z] = b_half
    a2buf[z, m] = a2send[z]
    a2_copies = [
        send(
            a2send.at[((me + d) % 16) // 4], a2buf.at[z, m], send16.at[1, d], recv16.at[1, d],
            (me + d) % 16,
        )
        for d in range(1, 16)
    ]
    b2_copies = [
        send(b2buf.at[z], b2buf.at[z], send4.at[4, d], recv4.at[4, d], same_m(d)) for d in range(1, 4)
    ]
    by_step = selection(128, lambda r: field(r, 2, 3, 5) + field(r, 0, 3, 3) + field(r, 4, 7, 0))
    for copy in a2_copies:
        copy.wait_recv()
    for k in range(4):
        a_scr[k * 8 : (k + 1) * 8] = dot(by_step, a2buf[k].reshape(128, 128)).reshape(8, 16, 128)
    for copy in b2_copies:
        copy.wait_recv()
    b_scr[...] = b2buf[...].astype(jnp.float32).reshape(b_scr.shape)

    def incoming(j, carry):
        jb, jr = j // 4, j % 4
        parts = [jnp.zeros((16, 128), jnp.float32) for _ in range(4)]
        for k in range(32):
            parts[k % 4] += a_scr[k] * b_scr[k // 8, jb, pl.ds(jr * 8 + k % 8, 1), :]
        mixed_scr[j] = (parts[0] + parts[1]) + (parts[2] + parts[3])
        return carry

    lax.fori_loop(0, 16, incoming, 0, unroll=4)
    done = finish_block(pair, gating, mixed_scr[...], mid2, out2)

    from_blocks = selection(
        256, lambda r: field(r, 2, 3, 6) + field(r, 0, 3, 4) + field(r, 6, 3, 2) + field(r, 4, 3, 0)
    )
    fsend[...] = dot(from_blocks, done).astype(jnp.bfloat16).reshape(4, 64, 128)
    fbuf[m] = fsend[m]
    f_copies = [
        send(fsend.at[(m + d) % 4], fbuf.at[m], send4.at[5, d], recv4.at[5, d], same_z(d))
        for d in range(1, 4)
    ]
    for copy in f_copies:
        copy.wait_recv()
    o_ref[...] = fbuf[...]
    for copy in started:
        copy.wait_send()


def blocks(*args):
    embedding, pair_state, norm_scale, former, latter = args[:5]
    samples = embedding.shape[0]
    rest = [a.reshape(1, -1) if a.ndim == 1 else a for a in args[5:]]
    operands = [
        embedding, norm_scale.reshape(1, -1), former.T, latter.T, pair_state.reshape(256, 128), *rest
    ]
    bf16, f32 = jnp.bfloat16, jnp.float32
    vmem = pl.BlockSpec(memory_space=pltpu.VMEM)
    out = pl.pallas_call(
        functools.partial(kernel, samples),
        out_shape=jax.ShapeDtypeStruct((4, 64, 128), bf16),
        in_specs=[pl.BlockSpec(memory_space=pl.ANY)] * len(operands),
        out_specs=vmem,
        scratch_shapes=[pltpu.VMEM(a.shape, a.dtype) for a in operands]
        + [
            pltpu.VMEM(embedding.shape, f32),
            pltpu.VMEM((4, 256, 128), bf16),
            pltpu.VMEM((4, 256, 128), bf16),
            pltpu.VMEM((4, 64, 128), bf16),
            pltpu.VMEM((4, 64, 128), bf16),
            pltpu.VMEM((8, 16, 16, 128), bf16),
            pltpu.VMEM((4, 128, 128), bf16),
            pltpu.VMEM((4, 32, 128), bf16),
            pltpu.VMEM((4, 4, 32, 128), bf16),
            pltpu.VMEM((32, 16, 128), f32),
            pltpu.VMEM((4, 4, 32, 128), f32),
            pltpu.VMEM((16, 16, 128), f32),
            pltpu.VMEM((4, 32, 128), bf16),
            pltpu.VMEM((4, 4, 32, 128), bf16),
            pltpu.VMEM((4, 128, 128), bf16),
            pltpu.VMEM((4, 64, 128), bf16),
            pltpu.VMEM((4, 64, 128), bf16),
            pltpu.SemaphoreType.DMA((6, 4)),
            pltpu.SemaphoreType.DMA((6, 4)),
            pltpu.SemaphoreType.DMA((2, 16)),
            pltpu.SemaphoreType.DMA((2, 16)),
            pltpu.SemaphoreType.DMA((len(operands),)),
        ],
        compiler_params=pltpu.CompilerParams(
            collective_id=0, has_side_effects=True, vmem_limit_bytes=60 * 1024 * 1024
        ),
    )(*operands)
    return out.reshape(4, 4, 4, 4, 128).transpose(1, 2, 0, 3, 4).reshape(pair_state.shape)


def fits_blocks(mesh, embedding, pair_state, former, edge_weight):
    return (
        mesh.shape["res"] == 16
        and pair_state.shape[1:] == (64, 128)
        and embedding.shape[0] // mesh.shape["groups"] == 256
        and former.shape[1] == 32
        and edge_weight.shape == (128, 256)
    )


def solution(mesh):
    in_specs = (
        P("groups", "res", None),
        P(("groups", "res"), None, None),
        P(),
        P(),
        P(),
        P(),
        P(),
        P(),
        P(),
        P(),
        P(),
        P(),
        P(),
        P(),
        P(),
        P(),
        P(),
    )
    out_specs = P(("groups", "res"), None, None)

    def program(*args):
        blocked = fits_blocks(mesh, args[0], args[1], args[3], args[8])
        return jax.shard_map(
            blocks if blocked else shards,
            mesh=mesh, in_specs=in_specs, out_specs=out_specs, check_vma=False,
        )(*args)

    return program
```

```python
import functools

import jax
import jax.numpy as jnp
from jax import lax
from jax.experimental import pallas as pl
from jax.experimental.pallas import tpu as pltpu
from jax.sharding import PartitionSpec as P


def layer_normalize(values, gain):
    mean_val = jnp.mean(values, axis=-1, keepdims=True)
    centred = values - mean_val
    variance = jnp.mean(centred * centred, axis=-1, keepdims=True)
    return centred / jnp.sqrt(variance + 1e-05) * gain


def project_in(pair_block, norm_gain, weight_in, weight_gate):
    hidden_width = weight_in.shape[1] // 4
    normed = layer_normalize(pair_block.astype(jnp.float32), norm_gain).astype(jnp.bfloat16)
    projected = jnp.einsum("abc,cd->abd", normed, weight_in, preferred_element_type=jnp.float32)
    edge_left = (
        jax.nn.sigmoid(projected[..., hidden_width : 2 * hidden_width])
        * projected[..., :hidden_width]
    ).astype(jnp.bfloat16)
    edge_right = (
        jax.nn.sigmoid(projected[..., 3 * hidden_width :])
        * projected[..., 2 * hidden_width : 3 * hidden_width]
    ).astype(jnp.bfloat16)
    gating = jax.nn.sigmoid(
        jnp.einsum("abc,cd->abd", normed, weight_gate, preferred_element_type=jnp.float32)
    )
    return (edge_left, edge_right, gating)


def apply_update(pair_block, gating, mixed_normed, weight_final):
    update = jnp.einsum(
        "abc,cd->abd", mixed_normed, weight_final, preferred_element_type=jnp.float32
    )
    return (pair_block.astype(jnp.float32) + gating * update).astype(jnp.bfloat16)


def shards(
    homolog_embedding,
    pair_state,
    homolog_norm_scale,
    former_operand_matrix,
    latter_operand_matrix,
    outer_mean_weight,
    outer_mean_bias,
    outgoing_input_gain,
    outgoing_edge_weight,
    outgoing_gate_weight,
    outgoing_product_gain,
    outgoing_output_weight,
    incoming_input_gain,
    incoming_edge_weight,
    incoming_gate_weight,
    incoming_product_gain,
    incoming_output_weight,
):
    sequence_rows = homolog_embedding.shape[0]
    alignment_normalized = layer_normalize(
        homolog_embedding.astype(jnp.float32), homolog_norm_scale
    ).astype(jnp.bfloat16)
    left_factor = jnp.einsum(
        "vfd,dl->vfl",
        alignment_normalized,
        former_operand_matrix,
        preferred_element_type=jnp.float32,
    ).astype(jnp.bfloat16)
    right_factor = jnp.einsum(
        "vfd,dl->vfl",
        alignment_normalized,
        latter_operand_matrix,
        preferred_element_type=jnp.float32,
    ).astype(jnp.bfloat16)
    outer = (
        jnp.einsum(
            "sip,sjq->ijpq",
            left_factor,
            lax.all_gather(right_factor, "res", axis=1, tiled=True),
            preferred_element_type=jnp.float32,
        )
        / sequence_rows
    )
    flattened = outer.reshape(outer.shape[0], outer.shape[1], -1).astype(jnp.bfloat16)
    outer_update = (
        jnp.einsum("ijr,rc->ijc", flattened, outer_mean_weight, preferred_element_type=jnp.float32)
        + outer_mean_bias
    )
    pair_one = (pair_state.astype(jnp.float32) + outer_update).astype(jnp.bfloat16)
    edge_left, edge_right, gating = project_in(
        pair_one, outgoing_input_gain, outgoing_edge_weight, outgoing_gate_weight
    )
    mixed = jnp.einsum(
        "ikc,jkc->ijc",
        edge_left,
        lax.all_gather(edge_right, "res", axis=0, tiled=True),
        preferred_element_type=jnp.float32,
    )
    mixed_normed = layer_normalize(mixed, outgoing_product_gain).astype(jnp.bfloat16)
    pair_two = apply_update(pair_one, gating, mixed_normed, outgoing_output_weight)
    in_left, in_right, in_gating = project_in(
        pair_two, incoming_input_gain, incoming_edge_weight, incoming_gate_weight
    )
    in_mixed = jnp.einsum(
        "kic,kjc->ijc",
        lax.all_to_all(in_left, "res", split_axis=1, concat_axis=0, tiled=True),
        lax.all_gather(in_right, "res", axis=0, tiled=True),
        preferred_element_type=jnp.float32,
    )
    in_normed = layer_normalize(in_mixed, incoming_product_gain).astype(jnp.bfloat16)
    return apply_update(pair_two, in_gating, in_normed, incoming_output_weight)


def sigmoid(values):
    return 1.0 / (1.0 + jnp.exp(-values))


def selection(size, source_row):
    out_row = lax.broadcasted_iota(jnp.int32, (size, size), 0)
    column = lax.broadcasted_iota(jnp.int32, (size, size), 1)
    return jnp.where(source_row(out_row) == column, 1.0, 0.0).astype(jnp.bfloat16)


def field(value, low, mask, to):
    return ((value >> low) & mask) << to


def dot(a, b):
    return jnp.dot(a, b, preferred_element_type=jnp.float32)


def packed(edges, top, bottom):
    low = lax.broadcasted_iota(jnp.int32, top.shape, 1) < edges
    first = jnp.where(low, top, pltpu.roll(bottom, edges, 1))
    second = jnp.where(low, pltpu.roll(top, edges, 1), bottom)
    return first.astype(jnp.bfloat16), second.astype(jnp.bfloat16)


def project_block(pair, gain, weight_in, weight_gate):
    h = weight_in.shape[1] // 4
    w = weight_in[...]
    normed = layer_normalize(pair, gain[...]).astype(jnp.bfloat16)
    values = dot(normed, jnp.concatenate([w[:, :h], w[:, 2 * h : 3 * h]], axis=1))
    gates = dot(normed, jnp.concatenate([w[:, h : 2 * h], w[:, 3 * h :]], axis=1))
    return sigmoid(gates) * values, sigmoid(dot(normed, weight_gate[...]))


def finish_block(pair, gating, mixed, gain, weight_out):
    h = gain.shape[1]
    mixed = mixed.reshape(pair.shape)
    mixed = (mixed + pltpu.roll(mixed, h, 1))[:, :h]
    normed = layer_normalize(mixed, gain[...]).astype(jnp.bfloat16)
    update = dot(normed, weight_out[...])
    return (pair + gating * update).astype(jnp.bfloat16)


def kernel(samples, *refs):
    count = (len(refs) - 23) // 2
    operands, o_ref, held, scratch = (
        refs[:count], refs[count], refs[count + 1 : 2 * count + 1], refs[2 * count + 1 :]
    )
    load_sem = scratch[-1]
    loads = [
        pltpu.make_async_copy(operand, here, load_sem.at[k])
        for k, (operand, here) in enumerate(zip(operands, held))
    ]
    for load in loads:
        load.start()
    body(samples, loads, *held, o_ref, *scratch[:-1])


def body(
    samples, loads,
    msa_ref, msa_gain, former, latter, pair_ref, outer_w, outer_b,
    gain1, edge1, gate1, mid1, out1,
    gain2, edge2, gate2, mid2, out2,
    o_ref,
    msa_scr, lbuf, rbuf, psend, pbuf, y_scr,
    abuf, bsend, bbuf, a_scr, b_scr, mixed_scr,
    a2send, a2buf, b2buf, fsend, fbuf,
    send4, recv4, send16, recv16,
):
    me = lax.axis_index("res")
    z, m = me // 4, me % 4
    barrier = pltpu.get_barrier_semaphore()
    for d in range(1, 16):
        pl.semaphore_signal(
            barrier, inc=1, device_id={"res": (me + d) % 16}, device_id_type=pl.DeviceIdType.MESH
        )

    started = []

    def send(src, dst, ssem, rsem, target):
        copy = pltpu.make_async_remote_copy(
            src_ref=src, dst_ref=dst, send_sem=ssem, recv_sem=rsem,
            device_id={"res": target}, device_id_type=pl.DeviceIdType.MESH,
        )
        copy.start()
        started.append(copy)
        return copy

    def same_z(d):
        return z * 4 + (m + d) % 4

    def same_m(d):
        return ((z + d) % 4) * 4 + m

    to_blocks = selection(
        256, lambda r: field(r, 6, 3, 2) + field(r, 4, 3, 4) + field(r, 2, 3, 0) + field(r, 0, 3, 6)
    )
    loads[4].wait()
    psend[...] = dot(to_blocks, pair_ref[...]).astype(jnp.bfloat16).reshape(4, 64, 128)
    pbuf[m] = psend[m]

    for load in loads[:4]:
        load.wait()
    msa_scr[...] = msa_ref[...].astype(jnp.float32)
    weights = jnp.concatenate([former[...]] * 4 + [latter[...]] * 4, axis=0)
    position = (lax.broadcasted_iota(jnp.int32, weights.shape, 0) >> 5) & 3
    factors = jnp.zeros((msa_ref.shape[0], 256), jnp.float32)
    for r in range(4):
        normed = layer_normalize(msa_scr[:, r, :], msa_gain[...]).astype(jnp.bfloat16)
        own = jnp.where(position == r, weights.astype(jnp.float32), 0.0).astype(jnp.bfloat16)
        factors += lax.dot_general(
            normed, own, (((1,), (1,)), ((), ())), preferred_element_type=jnp.float32
        )
    lbuf[m] = factors[:, :128].astype(jnp.bfloat16)
    rbuf[z] = factors[:, 128:].astype(jnp.bfloat16)

    pl.semaphore_wait(barrier, 15)
    for d in range(1, 4):
        send(rbuf.at[z], rbuf.at[z], send4.at[0, d], recv4.at[0, z], same_m(d))
    l_copies = [
        send(lbuf.at[m], lbuf.at[m], send4.at[1, d], recv4.at[1, d], same_z(d)) for d in range(1, 4)
    ]
    p_copies = [
        send(psend.at[(m + d) % 4], pbuf.at[m], send4.at[2, d], recv4.at[2, d], same_z(d))
        for d in range(1, 4)
    ]
    order_left = selection(
        512, lambda r: field(r, 2, 3, 7) + field(r, 0, 3, 5) + field(r, 4, 7, 2) + field(r, 7, 3, 0)
    )
    for copy in l_copies:
        copy.wait_recv()
    left_t = sum(
        lax.dot_general(
            order_left[:, k * 128 : (k + 1) * 128], lbuf[k], (((1,), (1,)), ((), ())),
            preferred_element_type=jnp.float32,
        )
        for k in range(4)
    ).astype(jnp.bfloat16)
    for copy in p_copies:
        copy.wait_recv()
    order_pair = selection(
        256, lambda r: field(r, 2, 3, 6) + field(r, 6, 3, 4) + field(r, 4, 3, 2) + field(r, 0, 3, 0)
    )
    state = dot(order_pair, pbuf[...].reshape(256, 128))

    near = jnp.where(z == 0, 1, z - 1)
    middle = jnp.where(z == 0, 2, jnp.where(z == 3, 1, z + 1))
    lane = lax.broadcasted_iota(jnp.int32, (128, 128), 1)
    for b in (z, near, middle, 6 - z - near - middle):
        if b is not z:
            pltpu.make_async_remote_copy(
                src_ref=rbuf.at[z], dst_ref=rbuf.at[b], send_sem=send4.at[0, 0],
                recv_sem=recv4.at[0, b], device_id={"res": b * 4 + m},
                device_id_type=pl.DeviceIdType.MESH,
            ).wait_recv()
        outer = dot(left_t, rbuf[b])
        x = [outer[k * 128 : (k + 1) * 128] for k in range(4)]
        low = lane < 64
        for u, v in ((0, 2), (1, 3)):
            x[u], x[v] = (
                jnp.where(low, x[u], pltpu.roll(x[v], 64, 1)),
                jnp.where(low, pltpu.roll(x[u], 64, 1), x[v]),
            )
        low = (lane & 32) == 0
        for u, v in ((0, 1), (2, 3)):
            x[u], x[v] = (
                jnp.where(low, x[u], pltpu.roll(x[v], 32, 1)),
                jnp.where(low, pltpu.roll(x[u], 96, 1), x[v]),
            )
        for k in range(4):
            y_scr[:, b * 4 + k] = (x[k] * (1.0 / samples)).astype(jnp.bfloat16).reshape(8, 16, 128)
    for load in loads[5:]:
        load.wait()
    update = sum(
        dot(y_scr[a].reshape(256, 128), outer_w[a * 128 : (a + 1) * 128, :]) for a in range(8)
    )
    pair = (state + (update + outer_b[...])).astype(jnp.bfloat16).astype(jnp.float32)

    edges, gating = project_block(pair, gain1, edge1, gate1)
    a_half, b_half = packed(64, edges[:128], edges[128:])
    to_rows = selection(128, lambda r: field(r, 2, 7, 4) + field(r, 5, 3, 2) + field(r, 0, 3, 0))
    bsend[...] = dot(to_rows, b_half).astype(jnp.bfloat16).reshape(4, 32, 128)
    abuf[m] = a_half
    bbuf[z, m] = bsend[m]
    b_copies = [
        send(bsend.at[(me + d) % 4], bbuf.at[z, m], send16.at[0, d], recv16.at[0, d], (me + d) % 16)
        for d in range(1, 16)
    ]
    a_copies = [
        send(abuf.at[m], abuf.at[m], send4.at[3, d], recv4.at[3, d], same_z(d)) for d in range(1, 4)
    ]
    for copy in a_copies + b_copies:
        copy.wait_recv()
    a_scr[...] = abuf[...].astype(jnp.float32).reshape(32, 16, 128)
    b_scr[...] = bbuf[...].astype(jnp.float32)

    def outgoing(j, carry):
        zj, rj = j // 4, j % 4
        parts = [jnp.zeros((16, 128), jnp.float32) for _ in range(4)]
        for k in range(32):
            parts[k % 4] += a_scr[k] * b_scr[zj, k // 8, pl.ds((k % 8) * 4 + rj, 1), :]
        mixed_scr[j] = (parts[0] + parts[1]) + (parts[2] + parts[3])
        return carry

    lax.fori_loop(0, 16, outgoing, 0, unroll=4)
    pair = finish_block(pair, gating, mixed_scr[...], mid1, out1).astype(jnp.float32)

    edges, gating = project_block(pair, gain2, edge2, gate2)
    halves = edges.reshape(16, 2, 8, 128)
    a_half, b_half = packed(64, halves[:, 0].reshape(128, 128), halves[:, 1].reshape(128, 128))
    a2send[...] = a_half.reshape(4, 32, 128)
    b2buf[z] = b_half
    a2buf[z, m] = a2send[z]
    a2_copies = [
        send(a2send.at[(z + d) % 4], a2buf.at[z, m], send4.at[6, d], recv4.at[6, d], same_m(d))
        for d in range(1, 4)
    ]
    b2_copies = [
        send(b2buf.at[z], b2buf.at[z], send4.at[4, d], recv4.at[4, d], same_m(d)) for d in range(1, 4)
    ]
    by_step = selection(128, lambda r: field(r, 2, 3, 5) + field(r, 0, 3, 3) + field(r, 4, 7, 0))
    for copy in a2_copies:
        copy.wait_recv()
    for copy in [
        send(a2buf.at[:, m], a2buf.at[:, m], send4.at[7, d], recv4.at[7, d], same_z(d))
        for d in range(1, 4)
    ]:
        copy.wait_recv()
    for k in range(4):
        a_scr[k * 8 : (k + 1) * 8] = dot(by_step, a2buf[k].reshape(128, 128)).reshape(8, 16, 128)
    for copy in b2_copies:
        copy.wait_recv()
    b_scr[...] = b2buf[...].astype(jnp.float32).reshape(b_scr.shape)

    def incoming(j, carry):
        jb, jr = j // 4, j % 4
        parts = [jnp.zeros((16, 128), jnp.float32) for _ in range(4)]
        for k in range(32):
            parts[k % 4] += a_scr[k] * b_scr[k // 8, jb, pl.ds(jr * 8 + k % 8, 1), :]
        mixed_scr[j] = (parts[0] + parts[1]) + (parts[2] + parts[3])
        return carry

    lax.fori_loop(0, 16, incoming, 0, unroll=4)
    done = finish_block(pair, gating, mixed_scr[...], mid2, out2)

    from_blocks = selection(
        256, lambda r: field(r, 2, 3, 6) + field(r, 0, 3, 4) + field(r, 6, 3, 2) + field(r, 4, 3, 0)
    )
    fsend[...] = dot(from_blocks, done).astype(jnp.bfloat16).reshape(4, 64, 128)
    fbuf[m] = fsend[m]
    f_copies = [
        send(fsend.at[(m + d) % 4], fbuf.at[m], send4.at[5, d], recv4.at[5, d], same_z(d))
        for d in range(1, 4)
    ]
    for copy in f_copies:
        copy.wait_recv()
    o_ref[...] = fbuf[...]
    for copy in started:
        copy.wait_send()


def blocks(*args):
    embedding, pair_state, norm_scale, former, latter = args[:5]
    samples = embedding.shape[0]
    rest = [a.reshape(1, -1) if a.ndim == 1 else a for a in args[5:]]
    operands = [
        embedding, norm_scale.reshape(1, -1), former.T, latter.T, pair_state.reshape(256, 128), *rest
    ]
    bf16, f32 = jnp.bfloat16, jnp.float32
    vmem = pl.BlockSpec(memory_space=pltpu.VMEM)
    out = pl.pallas_call(
        functools.partial(kernel, samples),
        out_shape=jax.ShapeDtypeStruct((4, 64, 128), bf16),
        in_specs=[pl.BlockSpec(memory_space=pl.ANY)] * len(operands),
        out_specs=vmem,
        scratch_shapes=[pltpu.VMEM(a.shape, a.dtype) for a in operands]
        + [
            pltpu.VMEM(embedding.shape, f32),
            pltpu.VMEM((4, 256, 128), bf16),
            pltpu.VMEM((4, 256, 128), bf16),
            pltpu.VMEM((4, 64, 128), bf16),
            pltpu.VMEM((4, 64, 128), bf16),
            pltpu.VMEM((8, 16, 16, 128), bf16),
            pltpu.VMEM((4, 128, 128), bf16),
            pltpu.VMEM((4, 32, 128), bf16),
            pltpu.VMEM((4, 4, 32, 128), bf16),
            pltpu.VMEM((32, 16, 128), f32),
            pltpu.VMEM((4, 4, 32, 128), f32),
            pltpu.VMEM((16, 16, 128), f32),
            pltpu.VMEM((4, 32, 128), bf16),
            pltpu.VMEM((4, 4, 32, 128), bf16),
            pltpu.VMEM((4, 128, 128), bf16),
            pltpu.VMEM((4, 64, 128), bf16),
            pltpu.VMEM((4, 64, 128), bf16),
            pltpu.SemaphoreType.DMA((8, 4)),
            pltpu.SemaphoreType.DMA((8, 4)),
            pltpu.SemaphoreType.DMA((1, 16)),
            pltpu.SemaphoreType.DMA((1, 16)),
            pltpu.SemaphoreType.DMA((len(operands),)),
        ],
        compiler_params=pltpu.CompilerParams(
            collective_id=0, has_side_effects=True, vmem_limit_bytes=60 * 1024 * 1024
        ),
    )(*operands)
    return out.reshape(4, 4, 4, 4, 128).transpose(1, 2, 0, 3, 4).reshape(pair_state.shape)


def fits_blocks(mesh, embedding, pair_state, former, edge_weight):
    return (
        mesh.shape["res"] == 16
        and pair_state.shape[1:] == (64, 128)
        and embedding.shape[0] // mesh.shape["groups"] == 256
        and former.shape[1] == 32
        and edge_weight.shape == (128, 256)
    )


def solution(mesh):
    in_specs = (
        P("groups", "res", None),
        P(("groups", "res"), None, None),
        P(),
        P(),
        P(),
        P(),
        P(),
        P(),
        P(),
        P(),
        P(),
        P(),
        P(),
        P(),
        P(),
        P(),
        P(),
    )
    out_specs = P(("groups", "res"), None, None)

    def program(*args):
        blocked = fits_blocks(mesh, args[0], args[1], args[3], args[8])
        return jax.shard_map(
            blocks if blocked else shards,
            mesh=mesh, in_specs=in_specs, out_specs=out_specs, check_vma=False,
        )(*args)

    return program
```
